1024 devices in a mesh: gx: 16 (over y, core), gy: 64 (over x, z).
Axes of the slice: x: 8, y: 8, z: 8, core: 2. Of those that a mesh axis runs over, the one named last changes fastest.
Arguments:
- kelvin_deviation: float32 [256, 4096, 128], P('gx', 'gy'), may hold values from -5 to 5
- vapour_content: float32 [256, 4096, 128], P('gx', 'gy'), may hold values from 0.05 to 0.5
- murky_sky_marker: int32 [256, 4096], P('gx', 'gy'), may hold values 0 or 1
- beam_incidence_ratio: bfloat16 [256, 4096], P('gx', 'gy'), may hold values from 0.099609375 to 1
- illuminated_profile_slots: int32 [16, 64, 1024], P('gx', 'gy'), may hold values from 0 to 1023, as said below
- illuminated_prefix_tally: int32 [16, 64], P('gx', 'gy'), may hold values from 0 to 1024, as said below
- uptake_coefficients: float32 [128, 128], replicated, may hold values from 0.002 to 0.2
- insolation_by_gpoint: float32 [128], replicated, may hold values from 0.02 to 0.1
Outputs:
- kelvin_after_step: float32 [256, 4096, 128], P('gx', 'gy')
- shortwave_gain_rate: float32 [256, 4096, 128], P('gx', 'gy')
The draws below stay inside these ranges and needn't reach their ends.
Inputs may be any that keep to these rules, and one draw needn't show every extreme that they name: `illuminated_profile_slots`: each device's entries are a permutation of its 1024 local column indices. `illuminated_prefix_tally`: each count is a multiple of 16; a device's count plus that of the device 8 away along gx (half the gx cycle) is at most 1024.
All inputs are finite; a program needn't handle non-finite values. No bound on the sum of `murky_sky_marker` on one device may be relied on, other than what follows from the above.
Results may differ from the reference program's by a relative error of at most 0.0027.
Values may be sent and summed in bfloat16 or wider, within the bound.
A program may use at most 32 MiB of HBM per device.

```python
import math
import jax
import jax.numpy as jnp
from jax import lax

VERTICAL_LAYERS = 128
GPOINTS = 128
CX = 16
CY = 64
TILE_SPANS_WEST = 256
TILE_SPANS_SOUTH = 4096
N_GX = 16
N_GY = 64


def draw_illuminated_prefix_tally(key, part):
    key = jax.random.fold_in(key, 11)
    share = CX * CY // N_GX
    subsolar = jax.random.randint(key, (1, N_GY), 0, N_GX)
    cycle_index = jnp.arange(N_GX, dtype=jnp.int32)[:, None]
    ahead = (cycle_index - subsolar) % N_GX
    distance = jnp.minimum(ahead, N_GX - ahead)
    per_peer = jnp.clip(share * (3 * N_GX - 8 * distance) // (2 * N_GX), 0, share)
    return (per_peer * N_GX).astype(jnp.int32)


def draw_illuminated_profile_slots(key, part):
    key = jax.random.fold_in(key, 23)
    device_keys = jax.random.split(key, N_GX * N_GY)

    def one_listing(single_key):
        return jax.random.permutation(single_key, CX * CY)
    listings = jax.vmap(one_listing)(device_keys)
    return listings.reshape(N_GX, N_GY, CX * CY).astype(jnp.int32)


def touch_ends(drawn, rng, smallest, largest):
    longest = drawn.shape.index(max(drawn.shape))
    spots = []
    for shift in (0, 1):
        where = [jax.random.randint(jax.random.fold_in(rng, axis), (), 0, length) for axis, length in enumerate(drawn.shape)]
        where[longest] = (where[longest] + shift) % drawn.shape[longest]
        spots.append(tuple(where))
    return drawn.at[spots[0]].set(smallest).at[spots[1]].set(largest)


def level_of(own_key, shape, cuts, low, high):
    loudness, own = 1.0, jax.random.fold_in(own_key, 6)
    for position, blocks in cuts:
        draws = jnp.exp(jax.random.uniform(jax.random.fold_in(own, position), (blocks,), jnp.float32, low / len(cuts), high / len(cuts)))
        loudness = loudness * jnp.repeat(draws, shape[position] // blocks).reshape([-1 if axis == position else 1 for axis in range(len(shape))])
    return loudness


def scatter_about(stream_key, extent, deviation, most, cuts=(), kind=jnp.bfloat16):
    gain = level_of(stream_key, extent, cuts, -0.22, 0.18) if cuts else 1.0
    values = jax.random.normal(stream_key, extent, jnp.float32) * deviation * gain
    return jnp.minimum(jnp.maximum(values, -most), most).astype(kind)


def setup_inputs(seed: int = 0) -> dict:
    streams_of = jax.random.split(jax.random.key(seed), 9)
    kelvin_deviation = scatter_about(streams_of[0], (TILE_SPANS_WEST, TILE_SPANS_SOUTH, VERTICAL_LAYERS), 1.0, 5.0, ((0, 16), (1, 64)), jnp.float32)
    vapour_content = jnp.clip(jnp.exp(math.log(0.5) - 2.3025851 * jax.random.uniform(streams_of[1], (TILE_SPANS_WEST, TILE_SPANS_SOUTH, VERTICAL_LAYERS), jnp.float32) ** level_of(streams_of[1], (TILE_SPANS_WEST, TILE_SPANS_SOUTH, VERTICAL_LAYERS), ((0, 16), (1, 64)), -0.2, 0.2)), 0.05, 0.5)
    murky_sky_marker = touch_ends((jax.random.randint(streams_of[2], (TILE_SPANS_WEST, TILE_SPANS_SOUTH), 0, 10) < 3).astype(jnp.int32), jax.random.fold_in(streams_of[2], 1), 0, 1)
    beam_incidence_ratio = jnp.clip(0.099609375 + 0.9003906 * jax.random.uniform(streams_of[3], (TILE_SPANS_WEST, TILE_SPANS_SOUTH), jnp.float32) ** level_of(streams_of[3], (TILE_SPANS_WEST, TILE_SPANS_SOUTH), ((0, 16), (1, 64)), -0.2, 0.2), 0.099609375, 1.0).astype(jnp.bfloat16)
    illuminated_profile_slots = draw_illuminated_profile_slots(jax.random.fold_in(streams_of[8], 71), 0)
    illuminated_prefix_tally = draw_illuminated_prefix_tally(jax.random.fold_in(streams_of[8], 71), 0)
    uptake_coefficients = jnp.clip(jnp.exp(jax.random.uniform(streams_of[6], (VERTICAL_LAYERS, GPOINTS), jnp.float32, math.log(0.002), math.log(0.2))), 0.002, 0.2)
    insolation_by_gpoint = jnp.clip(jax.random.uniform(streams_of[7], (GPOINTS,), jnp.float32, 0.02, 0.1), 0.02, 0.1)
    return dict(kelvin_deviation=kelvin_deviation, vapour_content=vapour_content, murky_sky_marker=murky_sky_marker, beam_incidence_ratio=beam_incidence_ratio, illuminated_profile_slots=illuminated_profile_slots, illuminated_prefix_tally=illuminated_prefix_tally, uptake_coefficients=uptake_coefficients, insolation_by_gpoint=insolation_by_gpoint)


def profile_ingredients(kelvin_deviation, vapour_content, murky_sky_marker):
    murky_scaling = 1.0 + 3.0 * murky_sky_marker.astype(jnp.float32)[..., None]
    return (vapour_content * murky_scaling * jnp.exp(0.25 * kelvin_deviation)).astype(jnp.bfloat16)


def radiate(retained_heat_gain, cosine, uptake_coefficients, insolation_by_gpoint):
    column_total, layer_tally = retained_heat_gain.shape
    tile_rows = math.gcd(column_total, 32)

    def tile_flux(pair):
        rows_here, cos_here = pair
        weighted = rows_here.astype(jnp.float32)[:, :, None] * uptake_coefficients[None, :, :]
        depth = jnp.cumsum(weighted, axis=1)
        return jnp.dot(jnp.exp(-depth / cos_here[:, None, None]), insolation_by_gpoint, precision=lax.Precision.HIGHEST)

    fluxes = lax.map(tile_flux, (retained_heat_gain.reshape(column_total // tile_rows, tile_rows, layer_tally), cosine.reshape(column_total // tile_rows, tile_rows))).reshape(column_total, layer_tally)
    incoming = jnp.broadcast_to(jnp.sum(insolation_by_gpoint), (column_total, 1))
    overhead = jnp.concatenate([incoming, fluxes[:, :-1]], axis=1)
    return cosine[:, None] * (overhead - fluxes)


def reference(kelvin_deviation, vapour_content, murky_sky_marker, beam_incidence_ratio, illuminated_profile_slots, illuminated_prefix_tally, uptake_coefficients, insolation_by_gpoint):
    westerly_span_size, southerly_span_size, layer_tally = kelvin_deviation.shape
    column_grid = CX * CY
    retained_heat_gain = profile_ingredients(kelvin_deviation, vapour_content, murky_sky_marker).reshape(westerly_span_size * southerly_span_size, layer_tally)
    cosine = beam_incidence_ratio.astype(jnp.float32).reshape(westerly_span_size * southerly_span_size)
    ranks = jnp.argsort(illuminated_profile_slots, axis=-1).astype(jnp.int32)
    lit_cells = (ranks < illuminated_prefix_tally[:, :, None]).astype(jnp.float32)
    lit_cells = lit_cells.reshape(N_GX, N_GY, CX, CY).transpose(0, 2, 1, 3).reshape(westerly_span_size * southerly_span_size)

    def device_block(pair):
        return radiate(pair[0], pair[1], uptake_coefficients, insolation_by_gpoint)

    heated = lax.map(device_block, (retained_heat_gain.reshape(-1, column_grid, layer_tally), cosine.reshape(-1, column_grid)))
    shortwave_gain_rate = (heated.reshape(westerly_span_size * southerly_span_size, layer_tally) * lit_cells[:, None]).reshape(westerly_span_size, southerly_span_size, layer_tally)
    adjacent_to_profile = jnp.roll(kelvin_deviation, 1, 0) + jnp.roll(kelvin_deviation, -1, 0) + jnp.roll(kelvin_deviation, 1, 1) + jnp.roll(kelvin_deviation, -1, 1)
    kelvin_after_step = kelvin_deviation + 0.2 * (adjacent_to_profile - 4.0 * kelvin_deviation) + shortwave_gain_rate
    return kelvin_after_step, shortwave_gain_rate
```

```python
import functools

import jax
import jax.numpy as jnp
from jax import lax
from jax.experimental import pallas as pl
from jax.experimental.pallas import tpu as pltpu
from jax.sharding import PartitionSpec as P

LOG2E = 1.4426950408889634
MESH = pl.DeviceIdType.MESH
NT = (((1,), (1,)), ((), ()))
F32, BF16, I32 = jnp.float32, jnp.bfloat16, jnp.int32
CX, CY, LEVELS = 16, 64, 128
CELLS = CX * CY
TILES = CELLS // 128
GROUP = 4
GROWS = 64
UNROLL = 32


def dot(a, b):
    return jnp.dot(a, b, preferred_element_type=F32)


def dot_nt(a, b):
    return lax.dot_general(a, b, NT, preferred_element_type=F32)


def lanes(x):
    x = x.reshape(TILES, 2, CY)
    return jnp.concatenate([x[:, 0], x[:, 1]], axis=-1)


def halves(x):
    high = x.astype(BF16)
    return high, (x - high.astype(F32)).astype(BF16)


def one_hot(rows, columns, ids):
    return lax.broadcasted_iota(I32, (rows, columns), 0) == ids


def kernel(
    kelvin, vapour, cloud, cosine, listing, count, uptake, insolation,
    after_out, heat_out,
    grid, vap, cloud_v, cos_v, list_v, count_v, up_v, ins_v,
    edge, ynear, up_t, w_t, absorb, flux, heat_v, after_v,
    in_sem, out_sem, send_sem, recv_sem,
):
    gx, gy = lax.axis_index("gx"), lax.axis_index("gy")
    nx, ny = lax.axis_size("gx"), lax.axis_size("gy")
    places = (
        (lax.rem(gx + 1, nx), gy),
        (lax.rem(gx + nx - 1, nx), gy),
        (gx, lax.rem(gy + 1, ny)),
        (gx, lax.rem(gy + ny - 1, ny)),
    )
    loads = [
        pltpu.make_async_copy(src, dst, in_sem.at[i])
        for i, (src, dst) in enumerate(
            (
                (uptake, up_v),
                (insolation, ins_v),
                (listing, list_v),
                (count, count_v),
                (cloud, cloud_v),
                (cosine, cos_v),
                (kelvin, grid.at[pl.ds(1, CX)]),
                (vapour, vap),
            )
        )
    ]
    for load in loads:
        load.start()
    barrier = pltpu.get_barrier_semaphore()
    for place in places:
        pl.semaphore_signal(barrier, inc=1, device_id=place, device_id_type=MESH)

    for load in loads[:6]:
        load.wait()
    mu = lanes(cos_v[...].astype(F32))
    speed = (-LOG2E) * (1.0 + 3.0 * lanes(cloud_v[...].astype(F32))) / mu
    ids = list_v[...]
    live = lax.broadcasted_iota(I32, (TILES, CELLS), 1) < count_v[...]
    high = (one_hot(TILES, CELLS, ids >> 7) & live).astype(F32).astype(BF16)
    low = one_hot(128, CELLS, ids & 127).astype(F32).astype(BF16)
    gain = dot_nt(high, low) * mu
    up_t[...] = up_v[...].T
    w_t[...] = jnp.broadcast_to(jnp.log2(ins_v[...]), (128, 128)).T

    for load in loads[6:]:
        load.wait()
    for x in range(CX):
        edge[0, pl.ds(x, 1), :] = grid[x + 1, pl.ds(CY - 1, 1), :]
        edge[1, pl.ds(x, 1), :] = grid[x + 1, pl.ds(0, 1), :]
    pl.semaphore_wait(barrier, 4)
    sources = (grid.at[CX], grid.at[1], edge.at[0], edge.at[1])
    targets = (grid.at[0], grid.at[CX + 1], ynear.at[0], ynear.at[1])
    sends = [
        pltpu.make_async_remote_copy(
            src_ref=sources[i],
            dst_ref=targets[i],
            send_sem=send_sem.at[i],
            recv_sem=recv_sem.at[i],
            device_id=places[i],
            device_id_type=MESH,
        )
        for i in range(4)
    ]
    for send in sends:
        send.start()

    eye = one_hot(128, 128, lax.broadcasted_iota(I32, (128, 128), 1)).astype(F32).astype(BF16)
    for t in range(TILES):
        warm = grid[2 * t + 1 : 2 * t + 3].reshape(128, LEVELS)
        amount = vap[2 * t : 2 * t + 2].reshape(128, LEVELS)
        plain = (amount * jnp.exp(0.25 * warm)).astype(BF16)
        absorb[t] = dot_nt(eye, plain) * speed[t : t + 1]

    def some_gpoints(q, p, first):
        at = pl.ds(pl.multiple_of(p * GROWS, GROWS), GROWS)
        start = w_t[at, :]

        def fold(e):
            return jnp.sum(e.reshape(GROWS // 8, 8, 128), axis=0)

        above = fold(jnp.exp2(start))
        for t in range(GROUP):
            flux[t, :8] = above if first else flux[t, :8] + above

        def levels(b, carry):
            ks, depth = carry
            depth = list(depth)
            for u in range(UNROLL):
                level = b * UNROLL + u
                kb = jnp.broadcast_to(ks[:, u : u + 1], (GROWS, 128))
                for t in range(GROUP):
                    row = absorb[q * GROUP + t, pl.ds(level, 1), :]
                    depth[t] = depth[t] + kb * row
                    total = fold(jnp.exp2(depth[t]))
                    to = (t, pl.ds(pl.multiple_of(level * 8 + 8, 8), 8), slice(None))
                    flux[to] = total if first else flux[to] + total
            return pltpu.roll(ks, 128 - UNROLL, 1), tuple(depth)

        lax.fori_loop(0, LEVELS // UNROLL, levels, (up_t[at, :], (start,) * GROUP))

    sums = one_hot(32, 256, lax.broadcasted_iota(I32, (32, 256), 1) >> 3).astype(F32).astype(BF16)
    yrow = lax.broadcasted_iota(I32, (CY, 128), 0)
    outs = []
    for q in range(TILES // GROUP):
        some_gpoints(q, 0, True)
        for p in range(1, 128 // GROWS):
            some_gpoints(q, p, False)
        if q == 0:
            for send in sends:
                send.wait()
        for t in range(GROUP):
            tile = q * GROUP + t
            parts = []
            for r in range(4):
                drop = flux[t, r * 256 : r * 256 + 256] - flux[t, r * 256 + 8 : r * 256 + 264]
                h, l = halves(drop)
                parts.append(dot(sums, h) + dot(sums, l))
            gained = (jnp.concatenate(parts, axis=0) * gain[tile : tile + 1]).T
            for i in range(2):
                x = 2 * tile + i
                here = grid[x + 1]
                south = jnp.where(yrow == 0, ynear[0, x : x + 1, :], pltpu.roll(here, 1, 0))
                north = jnp.where(yrow == CY - 1, ynear[1, x : x + 1, :], pltpu.roll(here, CY - 1, 0))
                near = grid[x + 2] + grid[x] + north + south
                heat = gained[i * CY : i * CY + CY]
                heat_v[x] = heat
                after_v[x] = here + 0.2 * (near - 4.0 * here) + heat
        for i, (src, dst) in enumerate(((after_v, after_out), (heat_v, heat_out))):
            span = pl.ds(q * 2 * GROUP, 2 * GROUP)
            out = pltpu.make_async_copy(src.at[span], dst.at[span], out_sem.at[2 * q + i])
            out.start()
            outs.append(out)
    for out in outs:
        out.wait()


def local(kelvin, vapour, cloud, cosine, listing, count, uptake, insolation):
    hbm = pl.BlockSpec(memory_space=pltpu.HBM)
    vmem = pltpu.VMEM
    block = jax.ShapeDtypeStruct((CX, CY, LEVELS), F32)
    return pl.pallas_call(
        kernel,
        out_shape=(block, block),
        in_specs=[hbm] * 8,
        out_specs=(hbm, hbm),
        scratch_shapes=[
            vmem((CX + 2, CY, LEVELS), F32),
            vmem((CX, CY, LEVELS), F32),
            vmem((CX, CY), I32),
            vmem((CX, CY), BF16),
            vmem((1, CELLS), I32),
            vmem((1, 1), I32),
            vmem((128, 128), F32),
            vmem((1, 128), F32),
            vmem((2, CX, LEVELS), F32),
            vmem((2, CX, LEVELS), F32),
            vmem((128, 128), F32),
            vmem((128, 128), F32),
            vmem((TILES, LEVELS, 128), F32),
            vmem((GROUP, 8 * LEVELS + 8, 128), F32),
            vmem((CX, CY, LEVELS), F32),
            vmem((CX, CY, LEVELS), F32),
            pltpu.SemaphoreType.DMA((8,)),
            pltpu.SemaphoreType.DMA((2 * TILES // GROUP,)),
            pltpu.SemaphoreType.DMA((4,)),
            pltpu.SemaphoreType.DMA((4,)),
        ],
        compiler_params=pltpu.CompilerParams(
            collective_id=0, has_side_effects=True, vmem_limit_bytes=60 * 2**20
        ),
        cost_estimate=pl.CostEstimate(
            flops=4 * CELLS * 128 * 128, bytes_accessed=2**21, transcendentals=CELLS * 128 * 128
        ),
    )(
        kelvin,
        vapour,
        cloud,
        cosine,
        listing.reshape(1, CELLS),
        count,
        uptake,
        insolation.reshape(1, 128),
    )


def solution(mesh):
    in_specs = (
        P("gx", "gy", None),
        P("gx", "gy", None),
        P("gx", "gy"),
        P("gx", "gy"),
        P("gx", "gy", None),
        P("gx", "gy"),
        P(),
        P(),
    )
    out_specs = (P("gx", "gy", None), P("gx", "gy", None))
    return jax.shard_map(local, mesh=mesh, in_specs=in_specs, out_specs=out_specs, check_vma=False)
```

```python
import functools

import jax
import jax.numpy as jnp
from jax import lax
from jax.experimental import pallas as pl
from jax.experimental.pallas import tpu as pltpu
from jax.sharding import PartitionSpec as P

LOG2E = 1.4426950408889634
MESH = pl.DeviceIdType.MESH
NT = (((1,), (1,)), ((), ()))
F32, BF16, I32 = jnp.float32, jnp.bfloat16, jnp.int32
CX, CY, LEVELS = 16, 64, 128
CELLS = CX * CY
TILES = CELLS // 128
GROUP = 4
GROWS = 64
PLANES = 8
UNROLL = 32


def dot(a, b):
    return jnp.dot(a, b, preferred_element_type=F32)


def dot_nt(a, b):
    return lax.dot_general(a, b, NT, preferred_element_type=F32)


def lanes(x):
    x = x.reshape(TILES, 2, CY)
    return jnp.concatenate([x[:, 0], x[:, 1]], axis=-1)


def halves(x):
    high = x.astype(BF16)
    return high, (x - high.astype(F32)).astype(BF16)


def one_hot(rows, columns, ids):
    return lax.broadcasted_iota(I32, (rows, columns), 0) == ids


def kernel(
    kelvin, vapour, cloud, cosine, listing, count, uptake, insolation,
    still_out, high_out, low_out,
    grid, vap, cloud_v, cos_v, list_v, count_v, up_v, ins_v,
    ynear, up_t, w_t, absorb, flux, high_v, low_v, still_v,
    in_sem, out_sem, send_sem, recv_sem,
):
    gx, gy = lax.axis_index("gx"), lax.axis_index("gy")
    nx, ny = lax.axis_size("gx"), lax.axis_size("gy")
    z = lax.rem(gy, PLANES)
    even, first = lax.rem(gx, 2) == 0, gy == 0
    late = (
        (z == 0) | (z == PLANES - 1),
        z >= 2,
        even & ((gx > 0) | first),
        even | ((gx == nx - 1) & (gy > 0)),
    )
    early = tuple(jnp.logical_not(x) for x in late)
    west, east = (lax.rem(gx + nx - 1, nx), gy), (lax.rem(gx + 1, nx), gy)
    south, north = (gx, lax.rem(gy + ny - 1, ny)), (gx, lax.rem(gy + 1, ny))
    neighbours = (north, south, west, east)
    mine = (kelvin.at[:, CY - 1], kelvin.at[:, 0], kelvin.at[0], kelvin.at[CX - 1])
    lands = (ynear.at[0], ynear.at[1], grid.at[CX + 1], grid.at[0])
    back = (1, 0, 3, 2)
    sends = [
        pltpu.make_async_remote_copy(
            src_ref=mine[i],
            dst_ref=lands[i],
            send_sem=send_sem.at[i],
            recv_sem=recv_sem.at[i],
            device_id=neighbours[i],
            device_id_type=MESH,
        )
        for i in range(4)
    ]
    barrier = pltpu.get_barrier_semaphore()

    def greet(i):
        pl.semaphore_signal(barrier, inc=1, device_id=neighbours[i], device_id_type=MESH)

    def send(i):
        sends[i].start()

    def answer(i):
        sends[back[i]].wait_recv()
        sends[i].start()

    def receive(i):
        sends[back[i]].wait_recv()

    def each(when, act, order=range(4)):
        for i in order:
            pl.when(when[i])(functools.partial(act, i))

    greeted = sum(x.astype(I32) for x in late)
    each(early, greet)
    pl.when(greeted > 0)(lambda: pl.semaphore_wait(barrier, greeted))
    each(late, send)
    loads = [
        pltpu.make_async_copy(src, dst, in_sem.at[i])
        for i, (src, dst) in enumerate(
            (
                (uptake, up_v),
                (insolation, ins_v),
                (listing, list_v),
                (count, count_v),
                (cloud, cloud_v),
                (cosine, cos_v),
                (kelvin, grid.at[pl.ds(1, CX)]),
                (vapour, vap),
            )
        )
    ]
    for load in loads:
        load.start()
    for load in loads[:6]:
        load.wait()
    mu = lanes(cos_v[...].astype(F32))
    speed = (-LOG2E) * (1.0 + 3.0 * lanes(cloud_v[...].astype(F32))) / mu
    ids = list_v[...]
    live = lax.broadcasted_iota(I32, (TILES, CELLS), 1) < count_v[...]
    high = (one_hot(TILES, CELLS, ids >> 7) & live).astype(F32).astype(BF16)
    low = one_hot(128, CELLS, ids & 127).astype(F32).astype(BF16)
    gain = dot_nt(high, low) * mu
    up_t[...] = up_v[...].T
    w_t[...] = jnp.broadcast_to(jnp.log2(ins_v[...]), (128, 128)).T

    for load in loads[6:]:
        load.wait()
    eye = one_hot(128, 128, lax.broadcasted_iota(I32, (128, 128), 1)).astype(F32).astype(BF16)
    for t in range(TILES):
        warm = grid[2 * t + 1 : 2 * t + 3].reshape(128, LEVELS)
        amount = vap[2 * t : 2 * t + 2].reshape(128, LEVELS)
        plain = (amount * jnp.exp(0.25 * warm)).astype(BF16)
        absorb[t] = dot_nt(eye, plain) * speed[t : t + 1]

    def some_gpoints(q, p, first):
        at = pl.ds(pl.multiple_of(p * GROWS, GROWS), GROWS)
        start = w_t[at, :]

        def fold(e):
            return jnp.sum(e.reshape(GROWS // 8, 8, 128), axis=0)

        above = fold(jnp.exp2(start))
        for t in range(GROUP):
            flux[t, :8] = above if first else flux[t, :8] + above

        def levels(b, carry):
            ks, depth = carry
            depth = list(depth)
            for u in range(UNROLL):
                level = b * UNROLL + u
                kb = jnp.broadcast_to(ks[:, u : u + 1], (GROWS, 128))
                for t in range(GROUP):
                    row = absorb[q * GROUP + t, pl.ds(level, 1), :]
                    depth[t] = depth[t] + kb * row
                    total = fold(jnp.exp2(depth[t]))
                    to = (t, pl.ds(pl.multiple_of(level * 8 + 8, 8), 8), slice(None))
                    flux[to] = total if first else flux[to] + total
            return pltpu.roll(ks, 128 - UNROLL, 1), tuple(depth)

        lax.fori_loop(0, LEVELS // UNROLL, levels, (up_t[at, :], (start,) * GROUP))

    sums = one_hot(32, 256, lax.broadcasted_iota(I32, (32, 256), 1) >> 3).astype(F32).astype(BF16)
    yrow = lax.broadcasted_iota(I32, (CY, 128), 0)
    outs = []
    for q in range(TILES // GROUP):
        some_gpoints(q, 0, True)
        for p in range(1, 128 // GROWS):
            some_gpoints(q, p, False)
        if q == 0:
            pl.when(z >= 2)(functools.partial(each, early, answer, (2, 3, 0, 1)))
        for t in range(GROUP):
            tile = q * GROUP + t
            parts = []
            for r in range(4):
                drop = flux[t, r * 256 : r * 256 + 256] - flux[t, r * 256 + 8 : r * 256 + 264]
                h, l = halves(drop)
                parts.append(dot(sums, h) + dot(sums, l))
            gained = (jnp.concatenate(parts, axis=0) * gain[tile : tile + 1]).T
            for i in range(2):
                x = 2 * tile + i
                here = grid[x + 1]
                near = jnp.where(yrow == 0, 0.0, pltpu.roll(here, 1, 0))
                near += jnp.where(yrow == CY - 1, 0.0, pltpu.roll(here, CY - 1, 0))
                if x > 0:
                    near += grid[x]
                if x < CX - 1:
                    near += grid[x + 2]
                high_v[x], low_v[x] = halves(gained[i * CY : i * CY + CY])
                still_v[x] = here + 0.2 * (near - 4.0 * here)
        span = pl.ds(q * 2 * GROUP, 2 * GROUP)
        for i, (src, dst) in enumerate(((high_v, high_out), (low_v, low_out))):
            out = pltpu.make_async_copy(src.at[span], dst.at[span], out_sem.at[2 * q + i])
            out.start()
            outs.append(out)
    pl.when(z < 2)(functools.partial(each, early, answer, (2, 3, 0, 1)))
    each(late, receive)
    still_v[0] += 0.2 * grid[0]
    still_v[CX - 1] += 0.2 * grid[CX + 1]
    for x in range(CX):
        still_v[x, :1] += 0.2 * ynear[0, x : x + 1]
        still_v[x, CY - 1 :] += 0.2 * ynear[1, x : x + 1]
    out = pltpu.make_async_copy(still_v, still_out, out_sem.at[2 * TILES // GROUP])
    out.start()
    for i in range(4):
        sends[i].wait_send()
    out.wait()
    for out in outs:
        out.wait()


def local(kelvin, vapour, cloud, cosine, listing, count, uptake, insolation):
    hbm = pl.BlockSpec(memory_space=pltpu.HBM)
    vmem = pltpu.VMEM
    block = (CX, CY, LEVELS)
    still, high, low = pl.pallas_call(
        kernel,
        out_shape=tuple(jax.ShapeDtypeStruct(block, x) for x in (F32, BF16, BF16)),
        in_specs=[hbm] * 8,
        out_specs=(hbm, hbm, hbm),
        scratch_shapes=[
            vmem((CX + 2, CY, LEVELS), F32),
            vmem((CX, CY, LEVELS), F32),
            vmem((CX, CY), I32),
            vmem((CX, CY), BF16),
            vmem((1, CELLS), I32),
            vmem((1, 1), I32),
            vmem((128, 128), F32),
            vmem((1, 128), F32),
            vmem((2, CX, LEVELS), F32),
            vmem((128, 128), F32),
            vmem((128, 128), F32),
            vmem((TILES, LEVELS, 128), F32),
            vmem((GROUP, 8 * LEVELS + 8, 128), F32),
            vmem(block, BF16),
            vmem(block, BF16),
            vmem(block, F32),
            pltpu.SemaphoreType.DMA((8,)),
            pltpu.SemaphoreType.DMA((2 * TILES // GROUP + 1,)),
            pltpu.SemaphoreType.DMA((4,)),
            pltpu.SemaphoreType.DMA((4,)),
        ],
        compiler_params=pltpu.CompilerParams(
            collective_id=0, has_side_effects=True, vmem_limit_bytes=60 * 2**20
        ),
        cost_estimate=pl.CostEstimate(
            flops=4 * CELLS * 128 * 128, bytes_accessed=2**21, transcendentals=CELLS * 128 * 128
        ),
    )(
        kelvin,
        vapour,
        cloud,
        cosine,
        listing.reshape(1, CELLS),
        count,
        uptake,
        insolation.reshape(1, 128),
    )
    heat = high.astype(F32) + low.astype(F32)
    return still + heat, heat


def solution(mesh):
    in_specs = (
        P("gx", "gy", None),
        P("gx", "gy", None),
        P("gx", "gy"),
        P("gx", "gy"),
        P("gx", "gy", None),
        P("gx", "gy"),
        P(),
        P(),
    )
    out_specs = (P("gx", "gy", None), P("gx", "gy", None))
    return jax.shard_map(local, mesh=mesh, in_specs=in_specs, out_specs=out_specs, check_vma=False)
```

```python
import functools

import jax
import jax.numpy as jnp
from jax import lax
from jax.experimental import pallas as pl
from jax.experimental.pallas import tpu as pltpu
from jax.sharding import PartitionSpec as P

LOG2E = 1.4426950408889634
MESH = pl.DeviceIdType.MESH
NT = (((1,), (1,)), ((), ()))
F32, BF16, I32 = jnp.float32, jnp.bfloat16, jnp.int32
CX, CY, LEVELS = 16, 64, 128
CELLS = CX * CY
TILES = CELLS // 128
GROUP = 4
GROWS = 64
PLANES = 8
PIECES = 4
UNROLL = 32


def dot(a, b):
    return jnp.dot(a, b, preferred_element_type=F32)


def dot_nt(a, b):
    return lax.dot_general(a, b, NT, preferred_element_type=F32)


def lanes(x):
    x = x.reshape(TILES, 2, CY)
    return jnp.concatenate([x[:, 0], x[:, 1]], axis=-1)


def halves(x):
    high = x.astype(BF16)
    return high, (x - high.astype(F32)).astype(BF16)


def one_hot(rows, columns, ids):
    return lax.broadcasted_iota(I32, (rows, columns), 0) == ids


def kernel(
    kelvin, vapour, cloud, cosine, listing, count, uptake, insolation,
    after_out, heat_out, south_out, north_out,
    grid, vap, cloud_v, cos_v, list_v, count_v, up_v, ins_v,
    up_t, w_t, absorb, flux, heat_v, after_v,
    in_sem, out_sem, send_sem, recv_sem, here_sem,
):
    gx, gy = lax.axis_index("gx"), lax.axis_index("gy")
    nx, ny = lax.axis_size("gx"), lax.axis_size("gy")
    z = lax.rem(gy, PLANES)
    even, first = lax.rem(gx, 2) == 0, gy == 0
    late = (
        (z == 0) | (z == PLANES - 1),
        z >= 2,
        even & ((gx > 0) | first),
        even | ((gx == nx - 1) & (gy > 0)),
    )
    early = tuple(jnp.logical_not(x) for x in late)
    west, east = (lax.rem(gx + nx - 1, nx), gy), (lax.rem(gx + 1, nx), gy)
    south, north = (gx, lax.rem(gy + ny - 1, ny)), (gx, lax.rem(gy + 1, ny))
    neighbours = (north, south, west, east)
    mine = (kelvin.at[:, CY - 1], kelvin.at[:, 0], kelvin.at[0], kelvin.at[CX - 1])
    lands = (south_out, north_out, grid.at[CX + 1], grid.at[0])
    back = (1, 0, 3, 2)
    sends = [
        pltpu.make_async_remote_copy(
            src_ref=mine[i],
            dst_ref=lands[i],
            send_sem=send_sem.at[i],
            recv_sem=recv_sem.at[i],
            device_id=neighbours[i],
            device_id_type=MESH,
        )
        for i in range(4)
    ]
    barrier = pltpu.get_barrier_semaphore()

    def greet(i):
        pl.semaphore_signal(barrier, inc=1, device_id=neighbours[i], device_id_type=MESH)

    def call(i):
        pl.semaphore_signal(
            here_sem.at[back[i]], inc=1, device_id=neighbours[i], device_id_type=MESH
        )

    def send(i):
        sends[i].start()

    def answer(i):
        pl.semaphore_wait(here_sem.at[i], 1)
        sends[i].start()

    def receive(i):
        sends[back[i]].wait_recv()

    def each(when, act, order=range(4)):
        for i in order:
            pl.when(when[i])(functools.partial(act, i))

    greeted = sum(x.astype(I32) for x in late)
    each(early, greet)
    pl.when(greeted > 0)(lambda: pl.semaphore_wait(barrier, greeted))
    each(late, call)
    each(late, send)
    loads = [
        pltpu.make_async_copy(src, dst, in_sem.at[i])
        for i, (src, dst) in enumerate(
            (
                (uptake, up_v),
                (insolation, ins_v),
                (listing, list_v),
                (count, count_v),
                (cloud, cloud_v),
                (cosine, cos_v),
                (kelvin, grid.at[pl.ds(1, CX)]),
                (vapour, vap),
            )
        )
    ]
    for load in loads:
        load.start()
    for load in loads[:6]:
        load.wait()
    mu = lanes(cos_v[...].astype(F32))
    speed = (-LOG2E) * (1.0 + 3.0 * lanes(cloud_v[...].astype(F32))) / mu
    ids = list_v[...]
    live = lax.broadcasted_iota(I32, (TILES, CELLS), 1) < count_v[...]
    high = (one_hot(TILES, CELLS, ids >> 7) & live).astype(F32).astype(BF16)
    low = one_hot(128, CELLS, ids & 127).astype(F32).astype(BF16)
    gain = dot_nt(high, low) * mu
    up_t[...] = up_v[...].T
    w_t[...] = jnp.broadcast_to(jnp.log2(ins_v[...]), (128, 128)).T

    for load in loads[6:]:
        load.wait()
    eye = one_hot(128, 128, lax.broadcasted_iota(I32, (128, 128), 1)).astype(F32).astype(BF16)
    for t in range(TILES):
        warm = grid[2 * t + 1 : 2 * t + 3].reshape(128, LEVELS)
        amount = vap[2 * t : 2 * t + 2].reshape(128, LEVELS)
        plain = (amount * jnp.exp(0.25 * warm)).astype(BF16)
        absorb[t] = dot_nt(eye, plain) * speed[t : t + 1]

    def some_gpoints(q, p, first):
        at = pl.ds(pl.multiple_of(p * GROWS, GROWS), GROWS)
        start = w_t[at, :]

        def fold(e):
            return jnp.sum(e.reshape(GROWS // 8, 8, 128), axis=0)

        above = fold(jnp.exp2(start))
        for t in range(GROUP):
            flux[t, :8] = above if first else flux[t, :8] + above

        def levels(b, carry):
            ks, depth = carry
            depth = list(depth)
            for u in range(UNROLL):
                level = b * UNROLL + u
                kb = jnp.broadcast_to(ks[:, u : u + 1], (GROWS, 128))
                for t in range(GROUP):
                    row = absorb[q * GROUP + t, pl.ds(level, 1), :]
                    depth[t] = depth[t] + kb * row
                    total = fold(jnp.exp2(depth[t]))
                    to = (t, pl.ds(pl.multiple_of(level * 8 + 8, 8), 8), slice(None))
                    flux[to] = total if first else flux[to] + total
            return pltpu.roll(ks, 128 - UNROLL, 1), tuple(depth)

        lax.fori_loop(0, LEVELS // UNROLL, levels, (up_t[at, :], (start,) * GROUP))

    sums = one_hot(32, 256, lax.broadcasted_iota(I32, (32, 256), 1) >> 3).astype(F32).astype(BF16)
    yrow = lax.broadcasted_iota(I32, (CY, 128), 0)
    outs = []
    for q in range(TILES // GROUP):
        some_gpoints(q, 0, True)
        for p in range(1, 128 // GROWS):
            some_gpoints(q, p, False)
        if q == 0:
            pl.when(gy > 0)(functools.partial(each, early, answer, (2, 3)))
            pl.when(z >= 2)(functools.partial(each, early, answer, (0, 1)))
        for t in range(GROUP):
            tile = q * GROUP + t
            parts = []
            for r in range(4):
                drop = flux[t, r * 256 : r * 256 + 256] - flux[t, r * 256 + 8 : r * 256 + 264]
                h, l = halves(drop)
                parts.append(dot(sums, h) + dot(sums, l))
            gained = (jnp.concatenate(parts, axis=0) * gain[tile : tile + 1]).T
            for i in range(2):
                x = 2 * tile + i
                here = grid[x + 1]
                near = jnp.where(yrow == 0, 0.0, pltpu.roll(here, 1, 0))
                near += jnp.where(yrow == CY - 1, 0.0, pltpu.roll(here, CY - 1, 0))
                if x > 0:
                    near += grid[x]
                if x < CX - 1:
                    near += grid[x + 2]
                heat = gained[i * CY : i * CY + CY]
                heat_v[x] = heat
                after_v[x] = here + 0.2 * (near - 4.0 * here) + heat
        span = pl.ds(q * 2 * GROUP, 2 * GROUP)
        out = pltpu.make_async_copy(heat_v.at[span], heat_out.at[span], out_sem.at[q])
        out.start()
        outs.append(out)
    pl.when(gy == 0)(functools.partial(each, early, answer, (2, 3)))
    receive(2)
    receive(3)
    after_v[0] += 0.2 * grid[0]
    after_v[CX - 1] += 0.2 * grid[CX + 1]
    out = pltpu.make_async_copy(after_v, after_out, out_sem.at[TILES // GROUP])
    out.start()
    outs.append(out)
    pl.when(z < 2)(functools.partial(each, early, answer, (0, 1)))
    receive(0)
    receive(1)
    for i in range(4):
        sends[i].wait_send()
    for out in outs:
        out.wait()


def finish(after, heat, south, north, after_out, heat_out, after_v, heat_v, edges, in_sem, out_sem):
    copy = pltpu.make_async_copy
    loads = [copy(south, edges.at[0], in_sem.at[0]), copy(north, edges.at[1], in_sem.at[1])]
    stores = []
    step = CX // PIECES
    for i in range(PIECES):
        span = pl.ds(i * step, step)
        loads.append(copy(after.at[span], after_v.at[span], in_sem.at[2 * i + 2]))
        loads.append(copy(heat.at[span], heat_v.at[span], in_sem.at[2 * i + 3]))
        stores.append(copy(after_v.at[span], after_out.at[span], out_sem.at[2 * i]))
        stores.append(copy(heat_v.at[span], heat_out.at[span], out_sem.at[2 * i + 1]))
    for load in loads:
        load.start()
    loads[0].wait()
    loads[1].wait()
    for i in range(PIECES):
        loads[2 * i + 2].wait()
        for x in range(i * step, i * step + step):
            after_v[x, :1] += 0.2 * edges[0, x : x + 1]
            after_v[x, CY - 1 :] += 0.2 * edges[1, x : x + 1]
        stores[2 * i].start()
        loads[2 * i + 3].wait()
        stores[2 * i + 1].start()
    for store in stores:
        store.wait()


def local(kelvin, vapour, cloud, cosine, listing, count, uptake, insolation):
    hbm = pl.BlockSpec(memory_space=pltpu.HBM)
    vmem = pltpu.VMEM
    block, edge = (CX, CY, LEVELS), (CX, LEVELS)
    after, heat, south, north = pl.pallas_call(
        kernel,
        out_shape=tuple(jax.ShapeDtypeStruct(x, F32) for x in (block, block, edge, edge)),
        in_specs=[hbm] * 8,
        out_specs=(hbm,) * 4,
        scratch_shapes=[
            vmem((CX + 2, CY, LEVELS), F32),
            vmem((CX, CY, LEVELS), F32),
            vmem((CX, CY), I32),
            vmem((CX, CY), BF16),
            vmem((1, CELLS), I32),
            vmem((1, 1), I32),
            vmem((128, 128), F32),
            vmem((1, 128), F32),
            vmem((128, 128), F32),
            vmem((128, 128), F32),
            vmem((TILES, LEVELS, 128), F32),
            vmem((GROUP, 8 * LEVELS + 8, 128), F32),
            vmem(block, F32),
            vmem(block, F32),
            pltpu.SemaphoreType.DMA((8,)),
            pltpu.SemaphoreType.DMA((TILES // GROUP + 1,)),
            pltpu.SemaphoreType.DMA((4,)),
            pltpu.SemaphoreType.DMA((4,)),
            pltpu.SemaphoreType.REGULAR((4,)),
        ],
        compiler_params=pltpu.CompilerParams(
            collective_id=0, has_side_effects=True, vmem_limit_bytes=60 * 2**20
        ),
        cost_estimate=pl.CostEstimate(
            flops=4 * CELLS * 128 * 128, bytes_accessed=2**21, transcendentals=CELLS * 128 * 128
        ),
    )(
        kelvin,
        vapour,
        cloud,
        cosine,
        listing.reshape(1, CELLS),
        count,
        uptake,
        insolation.reshape(1, 128),
    )
    return pl.pallas_call(
        finish,
        out_shape=tuple(jax.ShapeDtypeStruct(block, F32) for _ in range(2)),
        in_specs=[hbm] * 4,
        out_specs=(hbm,) * 2,
        scratch_shapes=[
            vmem(block, F32),
            vmem(block, F32),
            vmem((2, CX, LEVELS), F32),
            pltpu.SemaphoreType.DMA((2 * PIECES + 2,)),
            pltpu.SemaphoreType.DMA((2 * PIECES,)),
        ],
        compiler_params=pltpu.CompilerParams(vmem_limit_bytes=60 * 2**20),
    )(after, heat, south, north)


def solution(mesh):
    in_specs = (
        P("gx", "gy", None),
        P("gx", "gy", None),
        P("gx", "gy"),
        P("gx", "gy"),
        P("gx", "gy", None),
        P("gx", "gy"),
        P(),
        P(),
    )
    out_specs = (P("gx", "gy", None), P("gx", "gy", None))
    return jax.shard_map(local, mesh=mesh, in_specs=in_specs, out_specs=out_specs, check_vma=False)
```

```python
import functools

import jax
import jax.numpy as jnp
from jax import lax
from jax.experimental import pallas as pl
from jax.experimental.pallas import tpu as pltpu
from jax.sharding import PartitionSpec as P

LOG2E = 1.4426950408889634
MESH = pl.DeviceIdType.MESH
NT = (((1,), (1,)), ((), ()))
F32, BF16, I32 = jnp.float32, jnp.bfloat16, jnp.int32
CX, CY, LEVELS = 16, 64, 128
CELLS = CX * CY
TILES = CELLS // 128
GROUP = 4
GROWS = 64
PLANES = 8
PIECES = 2
UNROLL = 32


def dot(a, b):
    return jnp.dot(a, b, preferred_element_type=F32)


def dot_nt(a, b):
    return lax.dot_general(a, b, NT, preferred_element_type=F32)


def lanes(x):
    x = x.reshape(TILES, 2, CY)
    return jnp.concatenate([x[:, 0], x[:, 1]], axis=-1)


def halves(x):
    high = x.astype(BF16)
    return high, (x - high.astype(F32)).astype(BF16)


def one_hot(rows, columns, ids):
    return lax.broadcasted_iota(I32, (rows, columns), 0) == ids


def kernel(
    kelvin, vapour, cloud, cosine, listing, count, uptake, insolation,
    after_out, heat_out, south_out, north_out,
    grid, vap, cloud_v, cos_v, list_v, count_v, up_v, ins_v,
    up_t, w_t, absorb, flux, heat_v, after_v,
    in_sem, out_sem, send_sem, recv_sem, here_sem,
):
    gx, gy = lax.axis_index("gx"), lax.axis_index("gy")
    nx, ny = lax.axis_size("gx"), lax.axis_size("gy")
    z = lax.rem(gy, PLANES)
    even, first = lax.rem(gx, 2) == 0, gy == 0
    late = (
        (z == 0) | (z == PLANES - 1),
        z >= 2,
        even & (((gx > 0) & (gx <= nx // 2)) | ((gx == 0) & first)),
        even | ((gx > nx // 2) & ((gx < nx - 1) | (gy > 0))),
    )
    early = tuple(jnp.logical_not(x) for x in late)
    west, east = (lax.rem(gx + nx - 1, nx), gy), (lax.rem(gx + 1, nx), gy)
    south, north = (gx, lax.rem(gy + ny - 1, ny)), (gx, lax.rem(gy + 1, ny))
    neighbours = (north, south, west, east)
    mine = (kelvin.at[:, CY - 1], kelvin.at[:, 0], kelvin.at[0], kelvin.at[CX - 1])
    lands = (south_out, north_out, grid.at[CX + 1], grid.at[0])
    back = (1, 0, 3, 2)
    sends = [
        pltpu.make_async_remote_copy(
            src_ref=mine[i],
            dst_ref=lands[i],
            send_sem=send_sem.at[i],
            recv_sem=recv_sem.at[i],
            device_id=neighbours[i],
            device_id_type=MESH,
        )
        for i in range(4)
    ]
    barrier = pltpu.get_barrier_semaphore()

    def greet(i):
        pl.semaphore_signal(barrier, inc=1, device_id=neighbours[i], device_id_type=MESH)

    def call(i):
        pl.semaphore_signal(
            here_sem.at[back[i]], inc=1, device_id=neighbours[i], device_id_type=MESH
        )

    def send(i):
        sends[i].start()

    def answer(i):
        pl.semaphore_wait(here_sem.at[i], 1)
        sends[i].start()

    def receive(i):
        sends[back[i]].wait_recv()

    def each(when, act, order=range(4)):
        for i in order:
            pl.when(when[i])(functools.partial(act, i))

    greeted = sum(x.astype(I32) for x in late)
    each(early, greet)
    pl.when(greeted > 0)(lambda: pl.semaphore_wait(barrier, greeted))
    each(late, call)
    each(late, send)
    loads = [
        pltpu.make_async_copy(src, dst, in_sem.at[i])
        for i, (src, dst) in enumerate(
            (
                (uptake, up_v),
                (insolation, ins_v),
                (listing, list_v),
                (count, count_v),
                (cloud, cloud_v),
                (cosine, cos_v),
                (kelvin, grid.at[pl.ds(1, CX)]),
                (vapour, vap),
            )
        )
    ]
    for load in loads:
        load.start()
    for load in loads[:6]:
        load.wait()
    mu = lanes(cos_v[...].astype(F32))
    speed = (-LOG2E) * (1.0 + 3.0 * lanes(cloud_v[...].astype(F32))) / mu
    ids = list_v[...]
    live = lax.broadcasted_iota(I32, (TILES, CELLS), 1) < count_v[...]
    high = (one_hot(TILES, CELLS, ids >> 7) & live).astype(F32).astype(BF16)
    low = one_hot(128, CELLS, ids & 127).astype(F32).astype(BF16)
    gain = dot_nt(high, low) * mu
    up_t[...] = up_v[...].T
    w_t[...] = jnp.broadcast_to(jnp.log2(ins_v[...]), (128, 128)).T

    for load in loads[6:]:
        load.wait()
    eye = one_hot(128, 128, lax.broadcasted_iota(I32, (128, 128), 1)).astype(F32).astype(BF16)
    for t in range(TILES):
        warm = grid[2 * t + 1 : 2 * t + 3].reshape(128, LEVELS)
        amount = vap[2 * t : 2 * t + 2].reshape(128, LEVELS)
        plain = (amount * jnp.exp(0.25 * warm)).astype(BF16)
        absorb[t] = dot_nt(eye, plain) * speed[t : t + 1]

    def some_gpoints(q, p, first):
        at = pl.ds(pl.multiple_of(p * GROWS, GROWS), GROWS)
        start = w_t[at, :]

        def fold(e):
            return jnp.sum(e.reshape(GROWS // 8, 8, 128), axis=0)

        above = fold(jnp.exp2(start))
        for t in range(GROUP):
            flux[t, :8] = above if first else flux[t, :8] + above

        def levels(b, carry):
            ks, depth = carry
            depth = list(depth)
            for u in range(UNROLL):
                level = b * UNROLL + u
                kb = jnp.broadcast_to(ks[:, u : u + 1], (GROWS, 128))
                for t in range(GROUP):
                    row = absorb[q * GROUP + t, pl.ds(level, 1), :]
                    depth[t] = depth[t] + kb * row
                    total = fold(jnp.exp2(depth[t]))
                    to = (t, pl.ds(pl.multiple_of(level * 8 + 8, 8), 8), slice(None))
                    flux[to] = total if first else flux[to] + total
            return pltpu.roll(ks, 128 - UNROLL, 1), tuple(depth)

        lax.fori_loop(0, LEVELS // UNROLL, levels, (up_t[at, :], (start,) * GROUP))

    sums = one_hot(32, 256, lax.broadcasted_iota(I32, (32, 256), 1) >> 3).astype(F32).astype(BF16)
    yrow = lax.broadcasted_iota(I32, (CY, 128), 0)
    outs = []
    for q in range(TILES // GROUP):
        some_gpoints(q, 0, True)
        for p in range(1, 128 // GROWS):
            some_gpoints(q, p, False)
        if q == 0:
            pl.when(gy > 0)(functools.partial(each, early, answer, (2, 3)))
            pl.when(z >= 2)(functools.partial(each, early, answer, (0, 1)))
        for t in range(GROUP):
            tile = q * GROUP + t
            parts = []
            for r in range(4):
                drop = flux[t, r * 256 : r * 256 + 256] - flux[t, r * 256 + 8 : r * 256 + 264]
                h, l = halves(drop)
                parts.append(dot(sums, h) + dot(sums, l))
            gained = (jnp.concatenate(parts, axis=0) * gain[tile : tile + 1]).T
            for i in range(2):
                x = 2 * tile + i
                here = grid[x + 1]
                near = jnp.where(yrow == 0, 0.0, pltpu.roll(here, 1, 0))
                near += jnp.where(yrow == CY - 1, 0.0, pltpu.roll(here, CY - 1, 0))
                if x > 0:
                    near += grid[x]
                if x < CX - 1:
                    near += grid[x + 2]
                heat = gained[i * CY : i * CY + CY]
                heat_v[x] = heat
                after_v[x] = here + 0.2 * (near - 4.0 * here) + heat
        span = pl.ds(q * 2 * GROUP, 2 * GROUP)
        out = pltpu.make_async_copy(heat_v.at[span], heat_out.at[span], out_sem.at[q])
        out.start()
        outs.append(out)
    pl.when(gy == 0)(functools.partial(each, early, answer, (2, 3)))
    receive(2)
    receive(3)
    after_v[0] += 0.2 * grid[0]
    after_v[CX - 1] += 0.2 * grid[CX + 1]
    out = pltpu.make_async_copy(after_v, after_out, out_sem.at[TILES // GROUP])
    out.start()
    outs.append(out)
    pl.when(z < 2)(functools.partial(each, early, answer, (0, 1)))
    receive(0)
    receive(1)
    for i in range(4):
        sends[i].wait_send()
    for out in outs:
        out.wait()


def finish(after, heat, south, north, after_out, heat_out, after_v, heat_v, edges, in_sem, out_sem):
    copy = pltpu.make_async_copy
    loads = [copy(south, edges.at[0], in_sem.at[0]), copy(north, edges.at[1], in_sem.at[1])]
    stores = []
    step = CX // PIECES
    for i in range(PIECES):
        span = pl.ds(i * step, step)
        loads.append(copy(after.at[span], after_v.at[span], in_sem.at[2 * i + 2]))
        loads.append(copy(heat.at[span], heat_v.at[span], in_sem.at[2 * i + 3]))
        stores.append(copy(after_v.at[span], after_out.at[span], out_sem.at[2 * i]))
        stores.append(copy(heat_v.at[span], heat_out.at[span], out_sem.at[2 * i + 1]))
    for load in loads:
        load.start()
    loads[0].wait()
    loads[1].wait()
    for i in range(PIECES):
        loads[2 * i + 2].wait()
        for x in range(i * step, i * step + step):
            after_v[x, :1] += 0.2 * edges[0, x : x + 1]
            after_v[x, CY - 1 :] += 0.2 * edges[1, x : x + 1]
        stores[2 * i].start()
        loads[2 * i + 3].wait()
        stores[2 * i + 1].start()
    for store in stores:
        store.wait()


def local(kelvin, vapour, cloud, cosine, listing, count, uptake, insolation):
    hbm = pl.BlockSpec(memory_space=pltpu.HBM)
    vmem = pltpu.VMEM
    block, edge = (CX, CY, LEVELS), (CX, LEVELS)
    after, heat, south, north = pl.pallas_call(
        kernel,
        out_shape=tuple(jax.ShapeDtypeStruct(x, F32) for x in (block, block, edge, edge)),
        in_specs=[hbm] * 8,
        out_specs=(hbm,) * 4,
        scratch_shapes=[
            vmem((CX + 2, CY, LEVELS), F32),
            vmem((CX, CY, LEVELS), F32),
            vmem((CX, CY), I32),
            vmem((CX, CY), BF16),
            vmem((1, CELLS), I32),
            vmem((1, 1), I32),
            vmem((128, 128), F32),
            vmem((1, 128), F32),
            vmem((128, 128), F32),
            vmem((128, 128), F32),
            vmem((TILES, LEVELS, 128), F32),
            vmem((GROUP, 8 * LEVELS + 8, 128), F32),
            vmem(block, F32),
            vmem(block, F32),
            pltpu.SemaphoreType.DMA((8,)),
            pltpu.SemaphoreType.DMA((TILES // GROUP + 1,)),
            pltpu.SemaphoreType.DMA((4,)),
            pltpu.SemaphoreType.DMA((4,)),
            pltpu.SemaphoreType.REGULAR((4,)),
        ],
        compiler_params=pltpu.CompilerParams(
            collective_id=0, has_side_effects=True, vmem_limit_bytes=60 * 2**20
        ),
        cost_estimate=pl.CostEstimate(
            flops=4 * CELLS * 128 * 128, bytes_accessed=2**21, transcendentals=CELLS * 128 * 128
        ),
    )(
        kelvin,
        vapour,
        cloud,
        cosine,
        listing.reshape(1, CELLS),
        count,
        uptake,
        insolation.reshape(1, 128),
    )
    return pl.pallas_call(
        finish,
        out_shape=tuple(jax.ShapeDtypeStruct(block, F32) for _ in range(2)),
        in_specs=[hbm] * 4,
        out_specs=(hbm,) * 2,
        scratch_shapes=[
            vmem(block, F32),
            vmem(block, F32),
            vmem((2, CX, LEVELS), F32),
            pltpu.SemaphoreType.DMA((2 * PIECES + 2,)),
            pltpu.SemaphoreType.DMA((2 * PIECES,)),
        ],
        compiler_params=pltpu.CompilerParams(vmem_limit_bytes=60 * 2**20),
    )(after, heat, south, north)


def solution(mesh):
    in_specs = (
        P("gx", "gy", None),
        P("gx", "gy", None),
        P("gx", "gy"),
        P("gx", "gy"),
        P("gx", "gy", None),
        P("gx", "gy"),
        P(),
        P(),
    )
    out_specs = (P("gx", "gy", None), P("gx", "gy", None))
    return jax.shard_map(local, mesh=mesh, in_specs=in_specs, out_specs=out_specs, check_vma=False)
```

```python
import functools

import jax
import jax.numpy as jnp
from jax import lax
from jax.experimental import pallas as pl
from jax.experimental.pallas import tpu as pltpu
from jax.sharding import PartitionSpec as P

LOG2E = 1.4426950408889634
MESH = pl.DeviceIdType.MESH
NT = (((1,), (1,)), ((), ()))
F32, BF16, I32 = jnp.float32, jnp.bfloat16, jnp.int32
CX, CY, LEVELS = 16, 64, 128
CELLS = CX * CY
TILES = CELLS // 128
GROUP = 4
GROWS = 64
PLANES = 8
PIECES = 2
UNROLL = 32


def dot(a, b):
    return jnp.dot(a, b, preferred_element_type=F32)


def dot_nt(a, b):
    return lax.dot_general(a, b, NT, preferred_element_type=F32)


def lanes(x):
    x = x.reshape(TILES, 2, CY)
    return jnp.concatenate([x[:, 0], x[:, 1]], axis=-1)


def halves(x):
    high = x.astype(BF16)
    return high, (x - high.astype(F32)).astype(BF16)


def one_hot(rows, columns, ids):
    return lax.broadcasted_iota(I32, (rows, columns), 0) == ids


def kernel(
    kelvin, vapour, cloud, cosine, listing, count, uptake, insolation,
    after_out, heat_out, south_out, north_out,
    grid, vap, cloud_v, cos_v, list_v, count_v, up_v, ins_v,
    up_t, w_t, absorb, flux, heat_v, after_v,
    in_sem, out_sem, send_sem, recv_sem, here_sem,
):
    gx, gy = lax.axis_index("gx"), lax.axis_index("gy")
    nx, ny = lax.axis_size("gx"), lax.axis_size("gy")
    z = lax.rem(gy, PLANES)
    even, first = lax.rem(gx, 2) == 0, gy == 0
    start = (gx == 0) & first
    late = (
        (z == PLANES - 1) | start,
        (z >= 1) & jnp.logical_not((gx == 0) & (gy == 1)),
        even & (((gx > 0) & (gx <= nx // 2)) | start),
        even | ((gx > nx // 2) & ((gx < nx - 1) | (gy > 0))),
    )
    early = tuple(jnp.logical_not(x) for x in late)
    beside_west, beside_east = first & (gx == 1), first & (gx == nx - 1)
    west, east = (lax.rem(gx + nx - 1, nx), gy), (lax.rem(gx + 1, nx), gy)
    south, north = (gx, lax.rem(gy + ny - 1, ny)), (gx, lax.rem(gy + 1, ny))
    neighbours = (north, south, west, east)
    mine = (kelvin.at[:, CY - 1], kelvin.at[:, 0], kelvin.at[0], kelvin.at[CX - 1])
    lands = (south_out, north_out, grid.at[CX + 1], grid.at[0])
    back = (1, 0, 3, 2)
    sends = [
        pltpu.make_async_remote_copy(
            src_ref=mine[i],
            dst_ref=lands[i],
            send_sem=send_sem.at[i],
            recv_sem=recv_sem.at[i],
            device_id=neighbours[i],
            device_id_type=MESH,
        )
        for i in range(4)
    ]
    barrier = pltpu.get_barrier_semaphore()

    def greet(i):
        pl.semaphore_signal(barrier, inc=1, device_id=neighbours[i], device_id_type=MESH)

    def call(i):
        pl.semaphore_signal(
            here_sem.at[back[i]], inc=1, device_id=neighbours[i], device_id_type=MESH
        )

    def send(i):
        sends[i].start()

    def answer(i):
        pl.semaphore_wait(here_sem.at[i], 1)
        sends[i].start()

    def receive(i):
        sends[back[i]].wait_recv()

    def each(when, act, order=range(4)):
        for i in order:
            pl.when(when[i])(functools.partial(act, i))

    greeted = sum(x.astype(I32) for x in late)
    each(early, greet)
    pl.when(greeted > 0)(lambda: pl.semaphore_wait(barrier, greeted))
    each(late, call)
    each(late, send)
    loads = [
        pltpu.make_async_copy(src, dst, in_sem.at[i])
        for i, (src, dst) in enumerate(
            (
                (uptake, up_v),
                (insolation, ins_v),
                (listing, list_v),
                (count, count_v),
                (cloud, cloud_v),
                (cosine, cos_v),
                (kelvin, grid.at[pl.ds(1, CX)]),
                (vapour, vap),
            )
        )
    ]
    for load in loads:
        load.start()
    for load in loads[:6]:
        load.wait()
    mu = lanes(cos_v[...].astype(F32))
    speed = (-LOG2E) * (1.0 + 3.0 * lanes(cloud_v[...].astype(F32))) / mu
    ids = list_v[...]
    live = lax.broadcasted_iota(I32, (TILES, CELLS), 1) < count_v[...]
    high = (one_hot(TILES, CELLS, ids >> 7) & live).astype(F32).astype(BF16)
    low = one_hot(128, CELLS, ids & 127).astype(F32).astype(BF16)
    gain = dot_nt(high, low) * mu
    up_t[...] = up_v[...].T
    w_t[...] = jnp.broadcast_to(jnp.log2(ins_v[...]), (128, 128)).T

    for load in loads[6:]:
        load.wait()
    eye = one_hot(128, 128, lax.broadcasted_iota(I32, (128, 128), 1)).astype(F32).astype(BF16)
    for t in range(TILES):
        warm = grid[2 * t + 1 : 2 * t + 3].reshape(128, LEVELS)
        amount = vap[2 * t : 2 * t + 2].reshape(128, LEVELS)
        plain = (amount * jnp.exp(0.25 * warm)).astype(BF16)
        absorb[t] = dot_nt(eye, plain) * speed[t : t + 1]

    def some_gpoints(q, p, first):
        at = pl.ds(pl.multiple_of(p * GROWS, GROWS), GROWS)
        start = w_t[at, :]

        def fold(e):
            return jnp.sum(e.reshape(GROWS // 8, 8, 128), axis=0)

        above = fold(jnp.exp2(start))
        for t in range(GROUP):
            flux[t, :8] = above if first else flux[t, :8] + above

        def levels(b, carry):
            ks, depth = carry
            depth = list(depth)
            for u in range(UNROLL):
                level = b * UNROLL + u
                kb = jnp.broadcast_to(ks[:, u : u + 1], (GROWS, 128))
                for t in range(GROUP):
                    row = absorb[q * GROUP + t, pl.ds(level, 1), :]
                    depth[t] = depth[t] + kb * row
                    total = fold(jnp.exp2(depth[t]))
                    to = (t, pl.ds(pl.multiple_of(level * 8 + 8, 8), 8), slice(None))
                    flux[to] = total if first else flux[to] + total
            return pltpu.roll(ks, 128 - UNROLL, 1), tuple(depth)

        lax.fori_loop(0, LEVELS // UNROLL, levels, (up_t[at, :], (start,) * GROUP))

    sums = one_hot(32, 256, lax.broadcasted_iota(I32, (32, 256), 1) >> 3).astype(F32).astype(BF16)
    yrow = lax.broadcasted_iota(I32, (CY, 128), 0)
    outs = []
    for q in range(TILES // GROUP):
        some_gpoints(q, 0, True)
        for p in range(1, 128 // GROWS):
            some_gpoints(q, p, False)
        if q == 0:
            pl.when(jnp.logical_not(beside_west))(functools.partial(each, early, answer, (2,)))
            pl.when(jnp.logical_not(beside_east))(functools.partial(each, early, answer, (3,)))
            each(early, answer, (0,))
        for t in range(GROUP):
            tile = q * GROUP + t
            parts = []
            for r in range(4):
                drop = flux[t, r * 256 : r * 256 + 256] - flux[t, r * 256 + 8 : r * 256 + 264]
                h, l = halves(drop)
                parts.append(dot(sums, h) + dot(sums, l))
            gained = (jnp.concatenate(parts, axis=0) * gain[tile : tile + 1]).T
            for i in range(2):
                x = 2 * tile + i
                here = grid[x + 1]
                near = jnp.where(yrow == 0, 0.0, pltpu.roll(here, 1, 0))
                near += jnp.where(yrow == CY - 1, 0.0, pltpu.roll(here, CY - 1, 0))
                if x > 0:
                    near += grid[x]
                if x < CX - 1:
                    near += grid[x + 2]
                heat = gained[i * CY : i * CY + CY]
                heat_v[x] = heat
                after_v[x] = here + 0.2 * (near - 4.0 * here) + heat
        span = pl.ds(q * 2 * GROUP, 2 * GROUP)
        out = pltpu.make_async_copy(heat_v.at[span], heat_out.at[span], out_sem.at[q])
        out.start()
        outs.append(out)
    pl.when(beside_west)(functools.partial(each, early, answer, (2,)))
    pl.when(beside_east)(functools.partial(each, early, answer, (3,)))
    receive(2)
    receive(3)
    after_v[0] += 0.2 * grid[0]
    after_v[CX - 1] += 0.2 * grid[CX + 1]
    out = pltpu.make_async_copy(after_v, after_out, out_sem.at[TILES // GROUP])
    out.start()
    outs.append(out)
    each(early, answer, (1,))
    receive(0)
    receive(1)
    for i in range(4):
        sends[i].wait_send()
    for out in outs:
        out.wait()


def finish(after, heat, south, north, after_out, heat_out, after_v, heat_v, edges, in_sem, out_sem):
    copy = pltpu.make_async_copy
    loads = [copy(south, edges.at[0], in_sem.at[0]), copy(north, edges.at[1], in_sem.at[1])]
    stores = []
    step = CX // PIECES
    for i in range(PIECES):
        span = pl.ds(i * step, step)
        loads.append(copy(after.at[span], after_v.at[span], in_sem.at[2 * i + 2]))
        loads.append(copy(heat.at[span], heat_v.at[span], in_sem.at[2 * i + 3]))
        stores.append(copy(after_v.at[span], after_out.at[span], out_sem.at[2 * i]))
        stores.append(copy(heat_v.at[span], heat_out.at[span], out_sem.at[2 * i + 1]))
    for load in loads:
        load.start()
    loads[0].wait()
    loads[1].wait()
    for i in range(PIECES):
        loads[2 * i + 2].wait()
        for x in range(i * step, i * step + step):
            after_v[x, :1] += 0.2 * edges[0, x : x + 1]
            after_v[x, CY - 1 :] += 0.2 * edges[1, x : x + 1]
        stores[2 * i].start()
        loads[2 * i + 3].wait()
        stores[2 * i + 1].start()
    for store in stores:
        store.wait()


def local(kelvin, vapour, cloud, cosine, listing, count, uptake, insolation):
    hbm = pl.BlockSpec(memory_space=pltpu.HBM)
    vmem = pltpu.VMEM
    block, edge = (CX, CY, LEVELS), (CX, LEVELS)
    after, heat, south, north = pl.pallas_call(
        kernel,
        out_shape=tuple(jax.ShapeDtypeStruct(x, F32) for x in (block, block, edge, edge)),
        in_specs=[hbm] * 8,
        out_specs=(hbm,) * 4,
        scratch_shapes=[
            vmem((CX + 2, CY, LEVELS), F32),
            vmem((CX, CY, LEVELS), F32),
            vmem((CX, CY), I32),
            vmem((CX, CY), BF16),
            vmem((1, CELLS), I32),
            vmem((1, 1), I32),
            vmem((128, 128), F32),
            vmem((1, 128), F32),
            vmem((128, 128), F32),
            vmem((128, 128), F32),
            vmem((TILES, LEVELS, 128), F32),
            vmem((GROUP, 8 * LEVELS + 8, 128), F32),
            vmem(block, F32),
            vmem(block, F32),
            pltpu.SemaphoreType.DMA((8,)),
            pltpu.SemaphoreType.DMA((TILES // GROUP + 1,)),
            pltpu.SemaphoreType.DMA((4,)),
            pltpu.SemaphoreType.DMA((4,)),
            pltpu.SemaphoreType.REGULAR((4,)),
        ],
        compiler_params=pltpu.CompilerParams(
            collective_id=0, has_side_effects=True, vmem_limit_bytes=60 * 2**20
        ),
        cost_estimate=pl.CostEstimate(
            flops=4 * CELLS * 128 * 128, bytes_accessed=2**21, transcendentals=CELLS * 128 * 128
        ),
    )(
        kelvin,
        vapour,
        cloud,
        cosine,
        listing.reshape(1, CELLS),
        count,
        uptake,
        insolation.reshape(1, 128),
    )
    return pl.pallas_call(
        finish,
        out_shape=tuple(jax.ShapeDtypeStruct(block, F32) for _ in range(2)),
        in_specs=[hbm] * 4,
        out_specs=(hbm,) * 2,
        scratch_shapes=[
            vmem(block, F32),
            vmem(block, F32),
            vmem((2, CX, LEVELS), F32),
            pltpu.SemaphoreType.DMA((2 * PIECES + 2,)),
            pltpu.SemaphoreType.DMA((2 * PIECES,)),
        ],
        compiler_params=pltpu.CompilerParams(vmem_limit_bytes=60 * 2**20),
    )(after, heat, south, north)


def solution(mesh):
    in_specs = (
        P("gx", "gy", None),
        P("gx", "gy", None),
        P("gx", "gy"),
        P("gx", "gy"),
        P("gx", "gy", None),
        P("gx", "gy"),
        P(),
        P(),
    )
    out_specs = (P("gx", "gy", None), P("gx", "gy", None))
    return jax.shard_map(local, mesh=mesh, in_specs=in_specs, out_specs=out_specs, check_vma=False)
```

```python
import functools

import jax
import jax.numpy as jnp
from jax import lax
from jax.experimental import pallas as pl
from jax.experimental.pallas import tpu as pltpu
from jax.sharding import PartitionSpec as P

LOG2E = 1.4426950408889634
MESH = pl.DeviceIdType.MESH
NT = (((1,), (1,)), ((), ()))
F32, BF16, I32 = jnp.float32, jnp.bfloat16, jnp.int32
CX, CY, LEVELS = 16, 64, 128
CELLS = CX * CY
TILES = CELLS // 128
GROUP = 4
GROWS = 64
PLANES = 8
PIECES = 2
UNROLL = 32


def dot(a, b):
    return jnp.dot(a, b, preferred_element_type=F32)


def dot_nt(a, b):
    return lax.dot_general(a, b, NT, preferred_element_type=F32)


def lanes(x):
    x = x.reshape(TILES, 2, CY)
    return jnp.concatenate([x[:, 0], x[:, 1]], axis=-1)


def halves(x):
    high = x.astype(BF16)
    return high, (x - high.astype(F32)).astype(BF16)


def one_hot(rows, columns, ids):
    return lax.broadcasted_iota(I32, (rows, columns), 0) == ids


def kernel(
    kelvin, vapour, cloud, cosine, listing, count, uptake, insolation,
    after_out, heat_out, south_out, north_out,
    grid, vap, cloud_v, cos_v, list_v, count_v, up_v, ins_v,
    up_t, w_t, absorb, flux, heat_v, after_v,
    in_sem, out_sem, send_sem, recv_sem, here_sem,
):
    gx, gy = lax.axis_index("gx"), lax.axis_index("gy")
    nx, ny = lax.axis_size("gx"), lax.axis_size("gy")
    z = lax.rem(gy, PLANES)
    even, first = lax.rem(gx, 2) == 0, gy == 0
    start = (gx == 0) & first
    late = (
        (z == PLANES - 1) | start,
        (z >= 1) & jnp.logical_not((gx == 0) & (gy == 1)),
        even & (((gx > 0) & (gx <= nx // 2)) | start),
        even | ((gx > nx // 2) & ((gx < nx - 1) | (gy > 0))),
    )
    early = tuple(jnp.logical_not(x) for x in late)
    beside_west, beside_east = first & (gx == 1), first & (gx == nx - 1)
    west, east = (lax.rem(gx + nx - 1, nx), gy), (lax.rem(gx + 1, nx), gy)
    south, north = (gx, lax.rem(gy + ny - 1, ny)), (gx, lax.rem(gy + 1, ny))
    neighbours = (north, south, west, east)
    mine = (kelvin.at[:, CY - 1], kelvin.at[:, 0], kelvin.at[0], kelvin.at[CX - 1])
    lands = (south_out, north_out, grid.at[CX + 1], grid.at[0])
    back = (1, 0, 3, 2)
    inside = grid.at[pl.ds(1, CX)]
    loaded = (inside.at[:, CY - 1], inside.at[:, 0], inside.at[0], inside.at[CX - 1])
    sends, answers = (
        [
            pltpu.make_async_remote_copy(
                src_ref=edges[i],
                dst_ref=lands[i],
                send_sem=send_sem.at[i],
                recv_sem=recv_sem.at[i],
                device_id=neighbours[i],
                device_id_type=MESH,
            )
            for i in range(4)
        ]
        for edges in (mine, loaded)
    )
    barrier = pltpu.get_barrier_semaphore()

    def greet(i):
        pl.semaphore_signal(barrier, inc=1, device_id=neighbours[i], device_id_type=MESH)

    def call(i):
        pl.semaphore_signal(
            here_sem.at[back[i]], inc=1, device_id=neighbours[i], device_id_type=MESH
        )

    def send(i):
        sends[i].start()

    def answer(i):
        pl.semaphore_wait(here_sem.at[i], 1)
        answers[i].start()

    def receive(i):
        sends[back[i]].wait_recv()

    def each(when, act, order=range(4)):
        for i in order:
            pl.when(when[i])(functools.partial(act, i))

    greeted = sum(x.astype(I32) for x in late)
    each(early, greet)
    pl.when(greeted > 0)(lambda: pl.semaphore_wait(barrier, greeted))
    each(late, call)
    each(late, send)
    loads = [
        pltpu.make_async_copy(src, dst, in_sem.at[i])
        for i, (src, dst) in enumerate(
            (
                (uptake, up_v),
                (insolation, ins_v),
                (listing, list_v),
                (count, count_v),
                (cloud, cloud_v),
                (cosine, cos_v),
                (kelvin, grid.at[pl.ds(1, CX)]),
                (vapour, vap),
            )
        )
    ]
    for load in loads:
        load.start()
    for load in loads[:6]:
        load.wait()
    mu = lanes(cos_v[...].astype(F32))
    speed = (-LOG2E) * (1.0 + 3.0 * lanes(cloud_v[...].astype(F32))) / mu
    ids = list_v[...]
    live = lax.broadcasted_iota(I32, (TILES, CELLS), 1) < count_v[...]
    high = (one_hot(TILES, CELLS, ids >> 7) & live).astype(F32).astype(BF16)
    low = one_hot(128, CELLS, ids & 127).astype(F32).astype(BF16)
    gain = dot_nt(high, low) * mu
    up_t[...] = up_v[...].T
    w_t[...] = jnp.broadcast_to(jnp.log2(ins_v[...]), (128, 128)).T

    for load in loads[6:]:
        load.wait()
    eye = one_hot(128, 128, lax.broadcasted_iota(I32, (128, 128), 1)).astype(F32).astype(BF16)
    for t in range(TILES):
        warm = grid[2 * t + 1 : 2 * t + 3].reshape(128, LEVELS)
        amount = vap[2 * t : 2 * t + 2].reshape(128, LEVELS)
        plain = (amount * jnp.exp(0.25 * warm)).astype(BF16)
        absorb[t] = dot_nt(eye, plain) * speed[t : t + 1]

    def some_gpoints(q, p, first):
        at = pl.ds(pl.multiple_of(p * GROWS, GROWS), GROWS)
        start = w_t[at, :]

        def fold(e):
            return jnp.sum(e.reshape(GROWS // 8, 8, 128), axis=0)

        above = fold(jnp.exp2(start))
        for t in range(GROUP):
            flux[t, :8] = above if first else flux[t, :8] + above

        def levels(b, carry):
            ks, depth = carry
            depth = list(depth)
            for u in range(UNROLL):
                level = b * UNROLL + u
                kb = jnp.broadcast_to(ks[:, u : u + 1], (GROWS, 128))
                for t in range(GROUP):
                    row = absorb[q * GROUP + t, pl.ds(level, 1), :]
                    depth[t] = depth[t] + kb * row
                    total = fold(jnp.exp2(depth[t]))
                    to = (t, pl.ds(pl.multiple_of(level * 8 + 8, 8), 8), slice(None))
                    flux[to] = total if first else flux[to] + total
            return pltpu.roll(ks, 128 - UNROLL, 1), tuple(depth)

        lax.fori_loop(0, LEVELS // UNROLL, levels, (up_t[at, :], (start,) * GROUP))

    sums = one_hot(32, 256, lax.broadcasted_iota(I32, (32, 256), 1) >> 3).astype(F32).astype(BF16)
    yrow = lax.broadcasted_iota(I32, (CY, 128), 0)
    outs = []
    for q in range(TILES // GROUP):
        some_gpoints(q, 0, True)
        for p in range(1, 128 // GROWS):
            some_gpoints(q, p, False)
        if q == 0:
            pl.when(jnp.logical_not(beside_west))(functools.partial(each, early, answer, (2,)))
            pl.when(jnp.logical_not(beside_east))(functools.partial(each, early, answer, (3,)))
            each(early, answer, (0,))
        for t in range(GROUP):
            tile = q * GROUP + t
            parts = []
            for r in range(4):
                drop = flux[t, r * 256 : r * 256 + 256] - flux[t, r * 256 + 8 : r * 256 + 264]
                h, l = halves(drop)
                parts.append(dot(sums, h) + dot(sums, l))
            gained = (jnp.concatenate(parts, axis=0) * gain[tile : tile + 1]).T
            for i in range(2):
                x = 2 * tile + i
                here = grid[x + 1]
                near = jnp.where(yrow == 0, 0.0, pltpu.roll(here, 1, 0))
                near += jnp.where(yrow == CY - 1, 0.0, pltpu.roll(here, CY - 1, 0))
                if x > 0:
                    near += grid[x]
                if x < CX - 1:
                    near += grid[x + 2]
                heat = gained[i * CY : i * CY + CY]
                heat_v[x] = heat
                after_v[x] = here + 0.2 * (near - 4.0 * here) + heat
        span = pl.ds(q * 2 * GROUP, 2 * GROUP)
        out = pltpu.make_async_copy(heat_v.at[span], heat_out.at[span], out_sem.at[q])
        out.start()
        outs.append(out)
    pl.when(beside_west)(functools.partial(each, early, answer, (2,)))
    pl.when(beside_east)(functools.partial(each, early, answer, (3,)))
    receive(2)
    receive(3)
    after_v[0] += 0.2 * grid[0]
    after_v[CX - 1] += 0.2 * grid[CX + 1]
    out = pltpu.make_async_copy(after_v, after_out, out_sem.at[TILES // GROUP])
    out.start()
    outs.append(out)
    each(early, answer, (1,))
    receive(0)
    receive(1)
    for i in range(4):
        sends[i].wait_send()
    for out in outs:
        out.wait()


def finish(after, heat, south, north, after_out, heat_out, after_v, heat_v, edges, in_sem, out_sem):
    copy = pltpu.make_async_copy
    loads = [copy(south, edges.at[0], in_sem.at[0]), copy(north, edges.at[1], in_sem.at[1])]
    stores = []
    step = CX // PIECES
    for i in range(PIECES):
        span = pl.ds(i * step, step)
        loads.append(copy(after.at[span], after_v.at[span], in_sem.at[2 * i + 2]))
        loads.append(copy(heat.at[span], heat_v.at[span], in_sem.at[2 * i + 3]))
        stores.append(copy(after_v.at[span], after_out.at[span], out_sem.at[2 * i]))
        stores.append(copy(heat_v.at[span], heat_out.at[span], out_sem.at[2 * i + 1]))
    for load in loads:
        load.start()
    loads[0].wait()
    loads[1].wait()
    for i in range(PIECES):
        loads[2 * i + 2].wait()
        for x in range(i * step, i * step + step):
            after_v[x, :1] += 0.2 * edges[0, x : x + 1]
            after_v[x, CY - 1 :] += 0.2 * edges[1, x : x + 1]
        stores[2 * i].start()
        loads[2 * i + 3].wait()
        stores[2 * i + 1].start()
    for store in stores:
        store.wait()


def local(kelvin, vapour, cloud, cosine, listing, count, uptake, insolation):
    hbm = pl.BlockSpec(memory_space=pltpu.HBM)
    vmem = pltpu.VMEM
    block, edge = (CX, CY, LEVELS), (CX, LEVELS)
    after, heat, south, north = pl.pallas_call(
        kernel,
        out_shape=tuple(jax.ShapeDtypeStruct(x, F32) for x in (block, block, edge, edge)),
        in_specs=[hbm] * 8,
        out_specs=(hbm,) * 4,
        scratch_shapes=[
            vmem((CX + 2, CY, LEVELS), F32),
            vmem((CX, CY, LEVELS), F32),
            vmem((CX, CY), I32),
            vmem((CX, CY), BF16),
            vmem((1, CELLS), I32),
            vmem((1, 1), I32),
            vmem((128, 128), F32),
            vmem((1, 128), F32),
            vmem((128, 128), F32),
            vmem((128, 128), F32),
            vmem((TILES, LEVELS, 128), F32),
            vmem((GROUP, 8 * LEVELS + 8, 128), F32),
            vmem(block, F32),
            vmem(block, F32),
            pltpu.SemaphoreType.DMA((8,)),
            pltpu.SemaphoreType.DMA((TILES // GROUP + 1,)),
            pltpu.SemaphoreType.DMA((4,)),
            pltpu.SemaphoreType.DMA((4,)),
            pltpu.SemaphoreType.REGULAR((4,)),
        ],
        compiler_params=pltpu.CompilerParams(
            collective_id=0, has_side_effects=True, vmem_limit_bytes=60 * 2**20
        ),
        cost_estimate=pl.CostEstimate(
            flops=4 * CELLS * 128 * 128, bytes_accessed=2**21, transcendentals=CELLS * 128 * 128
        ),
    )(
        kelvin,
        vapour,
        cloud,
        cosine,
        listing.reshape(1, CELLS),
        count,
        uptake,
        insolation.reshape(1, 128),
    )
    return pl.pallas_call(
        finish,
        out_shape=tuple(jax.ShapeDtypeStruct(block, F32) for _ in range(2)),
        in_specs=[hbm] * 4,
        out_specs=(hbm,) * 2,
        scratch_shapes=[
            vmem(block, F32),
            vmem(block, F32),
            vmem((2, CX, LEVELS), F32),
            pltpu.SemaphoreType.DMA((2 * PIECES + 2,)),
            pltpu.SemaphoreType.DMA((2 * PIECES,)),
        ],
        compiler_params=pltpu.CompilerParams(vmem_limit_bytes=60 * 2**20),
    )(after, heat, south, north)


def solution(mesh):
    in_specs = (
        P("gx", "gy", None),
        P("gx", "gy", None),
        P("gx", "gy"),
        P("gx", "gy"),
        P("gx", "gy", None),
        P("gx", "gy"),
        P(),
        P(),
    )
    out_specs = (P("gx", "gy", None), P("gx", "gy", None))
    return jax.shard_map(local, mesh=mesh, in_specs=in_specs, out_specs=out_specs, check_vma=False)
```
